32 devices in a mesh: row: 8 (over z, y), col: 4 (over x, core).
Axes of the slice: x: 2, y: 2, z: 4, core: 2. Of those that a mesh axis runs over, the one named last changes fastest.
Arguments:
- hidden: bfloat16 [2048, 8192], P('row', 'col'), may hold values from -96 to 96
- norm_gain: bfloat16 [8192], P('col'), may hold values from 0.5 to 1.5
- w_query: bfloat16 [8192, 4096], P('row', 'col')
- w_key: bfloat16 [8192, 4096], P('row', 'col')
- w_value: bfloat16 [8192, 4096], P('row', 'col'), may hold values from -0.0625 to 0.0625
- w_out: bfloat16 [4096, 8192], P('row', 'col'), may hold values from -0.09375 to 0.09375
Outputs:
- context: bfloat16 [2048, 4096], P('row', 'col')
- layer_out: bfloat16 [2048, 8192], P('row', 'col')
The draws below stay inside these ranges and needn't reach their ends.
All inputs are finite; a program needn't handle non-finite values.
Results may differ from the reference program's by a relative error of at most 0.04.
Values may be sent and summed in bfloat16 or wider, within the bound.
No kernel may reach another device: no remote copies, remote signals or barrier semaphores. Data moves between devices by JAX's collectives and lax.ppermute only.
A program may use at most 128 MiB of HBM per device.

```python
import math
import jax
import jax.numpy as jnp
from jax import lax

D = 8192
HEADS = 32
HD = 128
SEQ = 2048
N_ROW = 8


def draw_hidden(key, part):
    row_key = jax.random.fold_in(key, 21)
    column_key = jax.random.fold_in(key, 22)
    entry_key = jax.random.fold_in(key, 23)
    position = jnp.arange(D, dtype=jnp.float32) / max(D - 1, 1)
    entries = jnp.clip(jax.random.normal(entry_key, (SEQ, D), jnp.float32), -6.0, 6.0)
    trend = 0.5
    rough = jax.random.uniform(column_key, (D,), jnp.float32, 0.0, 0.5)
    column = 0.3 * jnp.exp(math.log(10.0) * (trend * position + rough))
    row_scale = 0.3 * jnp.exp(math.log(10.0) * jax.random.uniform(row_key, (SEQ, 1), jnp.float32, 0.0, 1.0))
    return (entries * column[None, :] * row_scale).astype(jnp.bfloat16)


def shared_keys(key):
    base = jax.random.normal(jax.random.fold_in(key, 7), (D, HEADS * HD), jnp.float32)
    return jnp.clip(base, -6.0, 6.0) * math.sqrt(2.0 / D)


def draw_w_key(key, part):
    return shared_keys(key).astype(jnp.bfloat16)


def draw_w_query(key, part):
    own = jnp.clip(jax.random.normal(jax.random.fold_in(key, 8), (D, HEADS * HD), jnp.float32), -6.0, 6.0) * math.sqrt(2.0 / D)
    return own.astype(jnp.bfloat16)


def levels(stream_key, dims, shards, low, top_value):
    def one(dim, parts):
        draws = jax.random.uniform(jax.random.fold_in(jax.random.fold_in(stream_key, 6), dim), (parts,), jnp.float32, low / len(shards), top_value / len(shards))
        return jnp.repeat(jnp.exp(draws), dims[dim] // parts).reshape((-1,) + (1,) * (len(dims) - dim - 1))

    level = one(*shards[0])
    for cut in shards[1:]:
        level = level * one(*cut)
    return level


def gaussian(rng, dims, scale, most, cuts=(), kind=jnp.bfloat16):
    drawn = jax.random.normal(rng, dims, jnp.float32) * scale
    if len(cuts) > 0:
        drawn = levels(rng, dims, cuts, -0.22, 0.18) * drawn
    return jnp.clip(drawn, min=-most, max=most).astype(kind)


def setup_inputs(seed: int = 0) -> dict:
    arg_keys = jax.random.split(jax.random.key(seed), 7)
    return {
        "hidden": draw_hidden(jax.random.fold_in(arg_keys[6], 71), 0),
        "norm_gain": jnp.clip(1.0 + 0.1 * jax.random.normal(arg_keys[1], (D,), jnp.float32), 0.5, 1.5).astype(jnp.bfloat16),
        "w_query": draw_w_query(jax.random.fold_in(arg_keys[6], 71), 0),
        "w_key": draw_w_key(jax.random.fold_in(arg_keys[6], 71), 0),
        "w_value": gaussian(arg_keys[4], (D, HEADS * HD), D ** -0.5, 0.0625, ((0, 8), (1, 4))),
        "w_out": gaussian(arg_keys[5], (HEADS * HD, D), (HEADS * HD) ** -0.5, 0.09375, ((0, 8), (1, 4))),
    }


def rotary(values, positions):
    half = values.shape[-1] // 2
    freqs = jnp.exp(-math.log(10000.0) * 2.0 * jnp.arange(half, dtype=jnp.float32) / values.shape[-1])
    angles = positions.astype(jnp.float32)[:, None] * freqs[None, :]
    cosine = jnp.cos(angles)[:, None, :]
    sine = jnp.sin(angles)[:, None, :]
    first = values[..., :half]
    second = values[..., half:]
    return jnp.concatenate((first * cosine - second * sine, second * cosine + first * sine), axis=-1)

def blockwise(left, right):
    width = left.shape[1] // N_ROW
    total = jnp.zeros((left.shape[0], right.shape[1]), jnp.float32)
    for index in range(N_ROW):
        part = jnp.dot(left[:, index * width:(index + 1) * width], right[index * width:(index + 1) * width], preferred_element_type=jnp.float32)
        total = total + lax.optimization_barrier(part.astype(jnp.bfloat16)).astype(jnp.float32)
    return total

def one_head(operands):
    query, key, value = operands
    scores = jnp.dot(query, key.T, preferred_element_type=jnp.float32) * (1.0 / math.sqrt(HD))
    length = query.shape[0]
    allowed = jnp.arange(length, dtype=jnp.int32)[None, :] <= jnp.arange(length, dtype=jnp.int32)[:, None]
    scores = jnp.where(allowed, scores, -jnp.inf)
    peak = lax.optimization_barrier(jnp.max(scores, axis=1, keepdims=True))
    probs = jnp.exp(scores - peak)
    totals = lax.optimization_barrier(jnp.sum(probs, axis=1, keepdims=True))
    weighted = jnp.dot(probs.astype(jnp.bfloat16), value, preferred_element_type=jnp.float32)
    return (weighted / totals).astype(jnp.bfloat16)

def reference(hidden, norm_gain, w_query, w_key, w_value, w_out):
    residual = hidden.astype(jnp.float32)
    mean_square = lax.optimization_barrier(jnp.mean(residual * residual, axis=1, keepdims=True))
    normed = (residual * lax.rsqrt(mean_square + 1e-05) * norm_gain.astype(jnp.float32)[None, :]).astype(jnp.bfloat16)
    proj_q = blockwise(normed, w_query)
    proj_k = blockwise(normed, w_key)
    proj_v = blockwise(normed, w_value)
    length = hidden.shape[0]
    heads = w_query.shape[1] // HD
    positions = jnp.arange(length, dtype=jnp.int32)
    query = rotary(proj_q.reshape(length, heads, HD), positions).astype(jnp.bfloat16)
    key = rotary(proj_k.reshape(length, heads, HD), positions).astype(jnp.bfloat16)
    value = proj_v.astype(jnp.bfloat16).reshape(length, heads, HD)
    per_head = lax.map(one_head, (query.transpose(1, 0, 2), key.transpose(1, 0, 2), value.transpose(1, 0, 2)))
    context = per_head.transpose(1, 0, 2).reshape(length, heads * HD)
    attended = blockwise(context, w_out)
    layer_out = (residual + attended).astype(jnp.bfloat16)
    return (context, layer_out)
```

```python
import math

import jax
import jax.numpy as jnp
from jax import lax
from jax.experimental import pallas as pl
from jax.experimental.pallas import tpu as pltpu
from jax.sharding import PartitionSpec as P

HD = 128


norm_epsilon = 1e-05


def rotary(values, positions):
    half = values.shape[-1] // 2
    freqs = jnp.exp(
        -math.log(10000.0) * 2.0 * jnp.arange(half, dtype=jnp.float32) / values.shape[-1]
    )
    angles = positions.astype(jnp.float32)[:, None] * freqs[None, :]
    cosine = jnp.cos(angles)[:, None, :]
    sine = jnp.sin(angles)[:, None, :]
    first = values[..., :half]
    second = values[..., half:]
    return jnp.concatenate(
        (first * cosine - second * sine, second * cosine + first * sine), axis=-1
    )


def attend(carry, keys, values, queries, query_positions, key_positions, scale):
    peak, total, weighted = carry
    scores = jnp.einsum("qhd,khd->hqk", queries, keys, preferred_element_type=jnp.float32) * scale
    allowed = key_positions[None, :] <= query_positions[:, None]
    scores = jnp.where(allowed[None, :, :], scores, -jnp.inf)
    new_peak = jnp.maximum(peak, jnp.max(scores, axis=2))
    probs = jnp.exp(scores - new_peak[:, :, None])
    total = jnp.sum(probs, axis=2)
    weighted = jnp.einsum(
        "hqk,khd->hqd", probs.astype(jnp.bfloat16), values, preferred_element_type=jnp.float32
    )
    return (new_peak, total, weighted)


def start_state(heads_here, count):
    return (
        jnp.full((heads_here, count), -1e30, jnp.float32),
        jnp.zeros((heads_here, count), jnp.float32),
        jnp.zeros((heads_here, count, HD), jnp.float32),
    )


def finish(carry, count, heads_here):
    peak, total, weighted = carry
    return (
        (weighted / total[:, :, None])
        .transpose(1, 0, 2)
        .reshape(count, heads_here * HD)
        .astype(jnp.bfloat16)
    )


def on_device_any(hidden, norm_gain, w_query, w_key, w_value, w_out):
    rows = hidden.shape[0]
    features = hidden.shape[1] * lax.axis_size("col")
    residual = hidden.astype(jnp.float32)
    squares = lax.psum(jnp.sum(residual * residual, axis=1), "col")
    scaled = (
        residual
        * lax.rsqrt(squares / features + norm_epsilon)[:, None]
        * norm_gain.astype(jnp.float32)[None, :]
    )
    normed = lax.all_gather(scaled.astype(jnp.bfloat16), "col", axis=1, tiled=True)
    spread = lax.all_to_all(normed, "row", split_axis=1, concat_axis=0, tiled=True)
    joined = jnp.concatenate((w_query, w_key, w_value), axis=1)
    summed = lax.psum_scatter(
        jnp.dot(spread, joined, preferred_element_type=jnp.float32).astype(jnp.bfloat16),
        "row",
        scatter_dimension=0,
        tiled=True,
    ).astype(jnp.float32)
    proj_q, proj_k, proj_v = jnp.split(summed, 3, axis=1)
    heads_here = w_query.shape[1] // HD
    row_index = lax.axis_index("row")
    first_row = row_index * rows
    positions = first_row + jnp.arange(rows, dtype=jnp.int32)
    query = rotary(proj_q.reshape(rows, heads_here, HD), positions).astype(jnp.bfloat16)
    keys_here = (
        rotary(proj_k.reshape(rows, heads_here, HD), positions)
        .astype(jnp.bfloat16)
        .reshape(rows, heads_here * HD)
    )
    values_here = proj_v.astype(jnp.bfloat16)
    scale = 1.0 / math.sqrt(HD)
    initial = start_state(heads_here, rows)
    keys = lax.all_gather(keys_here, "row", axis=0, tiled=True).reshape(-1, heads_here, HD)
    values = lax.all_gather(values_here, "row", axis=0, tiled=True).reshape(-1, heads_here, HD)
    key_positions = jnp.arange(keys.shape[0], dtype=jnp.int32)
    folded = attend(initial, keys, values, query, positions, key_positions, scale)
    context = finish(folded, rows, heads_here)
    gathered_context = lax.all_gather(context, "col", axis=1, tiled=True)
    spread_context = lax.all_to_all(
        gathered_context, "row", split_axis=1, concat_axis=0, tiled=True
    )
    attended = lax.psum_scatter(
        jnp.dot(spread_context, w_out, preferred_element_type=jnp.float32).astype(jnp.bfloat16),
        "row",
        scatter_dimension=0,
        tiled=True,
    ).astype(jnp.float32)
    layer_out = (residual + attended).astype(jnp.bfloat16)
    return (context, layer_out)


def attention_kernel(block, q_ref, k_ref, v_ref, inv_ref, cos_ref, sin_ref, out_ref, keys, values):
    length = q_ref.shape[0]
    half = HD // 2
    factor = math.log2(math.e) / math.sqrt(HD)

    def turned(ref, at):
        raw = ref[at, :] * inv_ref[at, :]
        return (raw * cos_ref[at, :] + pltpu.roll(raw, half, 1) * sin_ref[at, :]).astype(
            jnp.bfloat16
        )

    for start in range(0, length, block):
        at = pl.ds(start, block)
        stop = start + block
        keys[at, :] = turned(k_ref, at)
        values[at, :] = (v_ref[at, :] * inv_ref[at, :]).astype(jnp.bfloat16)
        query = turned(q_ref, at)
        scores = lax.dot_general(
            query,
            keys[0:stop, :],
            (((1,), (1,)), ((), ())),
            preferred_element_type=jnp.float32,
        )
        row = lax.broadcasted_iota(jnp.int32, scores.shape, 0) + start
        column = lax.broadcasted_iota(jnp.int32, scores.shape, 1)
        scores = jnp.where(column <= row, scores, -jnp.inf)
        peak = jnp.max(scores, axis=1, keepdims=True)
        probs = jnp.exp2((scores - peak) * factor)
        total = jnp.sum(probs, axis=1, keepdims=True)
        weighted = jnp.dot(
            probs.astype(jnp.bfloat16), values[0:stop, :], preferred_element_type=jnp.float32
        )
        out_ref[at, :] = (weighted / total).astype(jnp.bfloat16)


def attention(query, key, value, inverse):
    length = query.shape[0]
    half = HD // 2
    freqs = jnp.exp(-math.log(10000.0) * 2.0 * jnp.arange(half, dtype=jnp.float32) / HD)
    angles = jnp.arange(length, dtype=jnp.int32).astype(jnp.float32)[:, None] * freqs[None, :]
    cosine = jnp.cos(angles)
    sine = jnp.sin(angles)
    whole = pl.BlockSpec(memory_space=pltpu.VMEM)
    return pl.pallas_call(
        lambda *refs: attention_kernel(min(256, length), *refs),
        out_shape=jax.ShapeDtypeStruct((length, HD), jnp.bfloat16),
        in_specs=[whole] * 6,
        out_specs=whole,
        scratch_shapes=[pltpu.VMEM((length, HD), jnp.bfloat16)] * 2,
        compiler_params=pltpu.CompilerParams(vmem_limit_bytes=48 * 1024 * 1024),
        cost_estimate=pl.CostEstimate(
            flops=2 * length * length * HD,
            bytes_accessed=16 * length * HD,
            transcendentals=length * length // 2,
        ),
    )(
        query,
        key,
        value,
        inverse,
        jnp.concatenate((cosine, cosine), axis=1),
        jnp.concatenate((-sine, sine), axis=1),
    )


def on_device_paired(hidden, norm_gain, w_query, w_key, w_value, w_out):
    rows, cols = lax.axis_size("row"), lax.axis_size("col")
    tokens = hidden.shape[0]
    length = tokens * rows
    row, col = lax.axis_index("row"), lax.axis_index("col")
    bits = {
        "y": (row & 1, "row", 1),
        "zl": ((row >> 1) & 1, "row", 2),
        "zh": ((row >> 2) & 1, "row", 4),
        "core": (col & 1, "col", 1),
        "x": ((col >> 1) & 1, "col", 2),
    }

    def swap(values, name):
        _, axis, step = bits[name]
        count = rows if axis == "row" else cols
        return lax.ppermute(values, axis, [(i, i ^ step) for i in range(count)])

    def parts(values, axis, name):
        bit = bits[name][0]
        keep = lax.dynamic_index_in_dim(values, bit, axis, keepdims=False)
        send = lax.dynamic_index_in_dim(values, 1 - bit, axis, keepdims=False)
        return keep, send

    def ordered(mine, other, name):
        low = bits[name][0] == 0
        return jnp.where(low, mine, other), jnp.where(low, other, mine)

    def joined(mine, other, name):
        return jnp.stack(ordered(mine, other, name))

    def deepened(weight):
        depth = weight.shape[0]
        split = weight.reshape(depth, 2, 2, 2 * HD)
        keep, send = parts(split, 2, "zl")
        return ordered(
            keep.reshape(depth, 4 * HD), swap(send, "zl").reshape(depth, 4 * HD), "zl"
        )

    weights = [deepened(w) for w in (w_value, w_key, w_query)]
    out_depth, out_width = w_out.shape
    keep, send = parts(w_out.reshape(out_depth, 2, out_width // 2), 1, "zl")
    weight_out = jnp.concatenate(ordered(keep, swap(send, "zl"), "zl"), axis=0)

    residual = hidden.astype(jnp.float32)
    squares = lax.all_gather(jnp.sum(residual * residual, axis=1), ("row", "col"))
    mean = jnp.sum(squares.reshape(rows, cols, tokens), axis=1) / (hidden.shape[1] * cols)
    inverse = lax.rsqrt(mean + norm_epsilon).reshape(length, 1)

    gained = (residual * norm_gain.astype(jnp.float32)[None, :]).astype(jnp.bfloat16)
    width = hidden.shape[1] // 2
    chunks = 4
    step = tokens // chunks
    collected = ([], [], [])
    for chunk in range(chunks):
        block = gained[chunk * step : (chunk + 1) * step].reshape(step, 2, width)
        keep, send = parts(block, 1, "y")
        block = joined(keep, swap(send, "y"), "y").reshape(2, 2, step // 2, width)
        keep, send = parts(block, 1, "x")
        block = joined(keep, swap(send, "x"), "x")
        keep, send = parts(block, 0, "zh")
        block = joined(keep, swap(send, "zh"), "zh")
        block = joined(block, swap(block, "zl"), "zl")
        block = joined(block, swap(block, "x"), "x").reshape(step * rows, width)
        first, second = ordered(block, swap(block, "core"), "core")
        for (low, high), results in zip(weights, collected):
            part = (
                jnp.dot(first, low, preferred_element_type=jnp.float32)
                + jnp.dot(second, high, preferred_element_type=jnp.float32)
            ).astype(jnp.bfloat16)
            keep, send = parts(part.reshape(step * rows, 2, 2 * HD), 1, "y")
            part = (keep.astype(jnp.float32) + swap(send, "y").astype(jnp.float32)).astype(
                jnp.bfloat16
            )
            keep, send = parts(part.reshape(step * rows, 2, HD), 1, "zh")
            part = keep.astype(jnp.float32) + swap(send, "zh").astype(jnp.float32)
            results.append(part.reshape(2, 2, 2, 2, step // 2, HD))

    def in_order(results):
        return jnp.stack(results).transpose(3, 2, 4, 0, 1, 5, 6).reshape(length, HD)

    value, key, query = (in_order(results) for results in collected)
    context = attention(query, key, value, inverse)

    blocks = context.reshape(rows, tokens, HD)
    home = jnp.zeros((tokens, rows, HD), jnp.bfloat16)
    for mask in range(rows):
        peer = row ^ mask
        block = lax.dynamic_index_in_dim(blocks, peer, 0, keepdims=False)
        if mask:
            block = lax.ppermute(block, "row", [(i, i ^ mask) for i in range(rows)])
        head = ((peer & 1) << 2) | (peer & 2) | (peer >> 2)
        home = lax.dynamic_update_slice_in_dim(home, block[:, None, :], head, 1)
    context_out = home.reshape(tokens, rows * HD)

    pieces = []
    for chunk in range(chunks):
        block = blocks[:, chunk * step : (chunk + 1) * step].reshape(rows, 2, step // 2, HD)
        keep, send = parts(block, 1, "x")
        block = joined(keep, swap(send, "x"), "x")
        keep, send = parts(block, 0, "zh")
        block = joined(keep, swap(send, "zh"), "zh")
        block = joined(block, swap(block, "zl"), "zl")
        block = joined(block, swap(block, "x"), "x")
        block = joined(block, swap(block, "core"), "core")
        block = block.transpose(4, 1, 5, 0, 2, 3, 6).reshape(rows * step, 8 * HD)
        part = jnp.dot(block, weight_out, preferred_element_type=jnp.float32).astype(jnp.bfloat16)
        part = part.reshape(4, 2, step, out_width // 2)
        keep, send = parts(part, 1, "y")
        part = (keep.astype(jnp.float32) + swap(send, "y").astype(jnp.float32)).astype(
            jnp.bfloat16
        )
        keep, send = parts(part.reshape(2, 2, step, out_width // 2), 0, "zh")
        part = (keep.astype(jnp.float32) + swap(send, "zh").astype(jnp.float32)).astype(
            jnp.bfloat16
        )
        keep, send = parts(part, 0, "zl")
        pieces.append(jnp.concatenate(ordered(keep, swap(send, "zl"), "zl"), axis=1))
    attended = jnp.concatenate(pieces, axis=0).astype(jnp.float32)
    layer_out = (residual + attended).astype(jnp.bfloat16)
    return (context_out, layer_out)


def on_device(hidden, norm_gain, w_query, w_key, w_value, w_out):
    rows, cols = lax.axis_size("row"), lax.axis_size("col")
    heads_here = w_query.shape[1] // HD
    paired = rows == 2**3 and cols == 2**2 and heads_here == rows and hidden.shape[0] % 64 == 0
    plan = on_device_paired if paired else on_device_any
    return plan(hidden, norm_gain, w_query, w_key, w_value, w_out)


def solution(mesh):
    placed = (
        P("row", "col"),
        P("col"),
        P("row", "col"),
        P("row", "col"),
        P("row", "col"),
        P("row", "col"),
    )
    return jax.shard_map(
        on_device,
        mesh=mesh,
        in_specs=placed,
        out_specs=(P("row", "col"), P("row", "col")),
        check_vma=False,
    )
```

```python
import math

import jax
import jax.numpy as jnp
from jax import lax
from jax.experimental import pallas as pl
from jax.experimental.pallas import tpu as pltpu
from jax.sharding import PartitionSpec as P

HD = 128


norm_epsilon = 1e-05

X, CORE, ZH, ZL, Y = range(5)


def rotary(values, positions):
    half = values.shape[-1] // 2
    freqs = jnp.exp(
        -math.log(10000.0) * 2.0 * jnp.arange(half, dtype=jnp.float32) / values.shape[-1]
    )
    angles = positions.astype(jnp.float32)[:, None] * freqs[None, :]
    cosine = jnp.cos(angles)[:, None, :]
    sine = jnp.sin(angles)[:, None, :]
    first = values[..., :half]
    second = values[..., half:]
    return jnp.concatenate(
        (first * cosine - second * sine, second * cosine + first * sine), axis=-1
    )


def attend(carry, keys, values, queries, query_positions, key_positions, scale):
    peak, total, weighted = carry
    scores = jnp.einsum("qhd,khd->hqk", queries, keys, preferred_element_type=jnp.float32) * scale
    allowed = key_positions[None, :] <= query_positions[:, None]
    scores = jnp.where(allowed[None, :, :], scores, -jnp.inf)
    new_peak = jnp.maximum(peak, jnp.max(scores, axis=2))
    probs = jnp.exp(scores - new_peak[:, :, None])
    total = jnp.sum(probs, axis=2)
    weighted = jnp.einsum(
        "hqk,khd->hqd", probs.astype(jnp.bfloat16), values, preferred_element_type=jnp.float32
    )
    return (new_peak, total, weighted)


def start_state(heads_here, count):
    return (
        jnp.full((heads_here, count), -1e30, jnp.float32),
        jnp.zeros((heads_here, count), jnp.float32),
        jnp.zeros((heads_here, count, HD), jnp.float32),
    )


def finish(carry, count, heads_here):
    peak, total, weighted = carry
    return (
        (weighted / total[:, :, None])
        .transpose(1, 0, 2)
        .reshape(count, heads_here * HD)
        .astype(jnp.bfloat16)
    )


def on_device_any(hidden, norm_gain, w_query, w_key, w_value, w_out):
    rows = hidden.shape[0]
    features = hidden.shape[1] * lax.axis_size("col")
    residual = hidden.astype(jnp.float32)
    squares = lax.psum(jnp.sum(residual * residual, axis=1), "col")
    scaled = (
        residual
        * lax.rsqrt(squares / features + norm_epsilon)[:, None]
        * norm_gain.astype(jnp.float32)[None, :]
    )
    normed = lax.all_gather(scaled.astype(jnp.bfloat16), "col", axis=1, tiled=True)
    spread = lax.all_to_all(normed, "row", split_axis=1, concat_axis=0, tiled=True)
    joined = jnp.concatenate((w_query, w_key, w_value), axis=1)
    summed = lax.psum_scatter(
        jnp.dot(spread, joined, preferred_element_type=jnp.float32).astype(jnp.bfloat16),
        "row",
        scatter_dimension=0,
        tiled=True,
    ).astype(jnp.float32)
    proj_q, proj_k, proj_v = jnp.split(summed, 3, axis=1)
    heads_here = w_query.shape[1] // HD
    row_index = lax.axis_index("row")
    first_row = row_index * rows
    positions = first_row + jnp.arange(rows, dtype=jnp.int32)
    query = rotary(proj_q.reshape(rows, heads_here, HD), positions).astype(jnp.bfloat16)
    keys_here = (
        rotary(proj_k.reshape(rows, heads_here, HD), positions)
        .astype(jnp.bfloat16)
        .reshape(rows, heads_here * HD)
    )
    values_here = proj_v.astype(jnp.bfloat16)
    scale = 1.0 / math.sqrt(HD)
    initial = start_state(heads_here, rows)
    keys = lax.all_gather(keys_here, "row", axis=0, tiled=True).reshape(-1, heads_here, HD)
    values = lax.all_gather(values_here, "row", axis=0, tiled=True).reshape(-1, heads_here, HD)
    key_positions = jnp.arange(keys.shape[0], dtype=jnp.int32)
    folded = attend(initial, keys, values, query, positions, key_positions, scale)
    context = finish(folded, rows, heads_here)
    gathered_context = lax.all_gather(context, "col", axis=1, tiled=True)
    spread_context = lax.all_to_all(
        gathered_context, "row", split_axis=1, concat_axis=0, tiled=True
    )
    attended = lax.psum_scatter(
        jnp.dot(spread_context, w_out, preferred_element_type=jnp.float32).astype(jnp.bfloat16),
        "row",
        scatter_dimension=0,
        tiled=True,
    ).astype(jnp.float32)
    layer_out = (residual + attended).astype(jnp.bfloat16)
    return (context, layer_out)


def attention_kernel(marks, q_ref, k_ref, v_ref, inv_ref, cos_ref, sin_ref, out_ref, query, keys, values):
    half = HD // 2
    slots, part = q_ref.shape[0], q_ref.shape[1]
    per_row = 4
    block = part * per_row
    factor = math.log2(math.e) / math.sqrt(HD)

    def turned(raw, at):
        return (raw * cos_ref[at, :] + pltpu.roll(raw, half, 1) * sin_ref[at, :]).astype(
            jnp.bfloat16
        )

    for row in range(slots // per_row):
        zh, zl, y = row >> 2, (row >> 1) & 1, row & 1
        for piece in range(per_row):
            h, j = piece >> 1, piece & 1
            slot = ((zh ^ marks[ZH]) * 2 + j) * 2 + (h ^ marks[X])
            slot = (slot * 2 + (zl ^ marks[ZL])) * 2 + y
            at = pl.ds(row * block + piece * part, part)
            inverse = inv_ref[at, :]
            query[at, :] = turned(q_ref[slot] * inverse, at)
            keys[at, :] = turned(k_ref[slot] * inverse, at)
            values[at, :] = (v_ref[slot] * inverse).astype(jnp.bfloat16)
        start, stop = row * block, (row + 1) * block
        scores = lax.dot_general(
            query[start:stop, :],
            keys[0:stop, :],
            (((1,), (1,)), ((), ())),
            preferred_element_type=jnp.float32,
        )
        down = lax.broadcasted_iota(jnp.int32, scores.shape, 0) + start
        along = lax.broadcasted_iota(jnp.int32, scores.shape, 1)
        scores = jnp.where(along <= down, scores, -jnp.inf)
        peak = jnp.max(scores, axis=1, keepdims=True)
        probs = jnp.exp2((scores - peak) * factor)
        total = jnp.sum(probs, axis=1, keepdims=True)
        weighted = jnp.dot(
            probs.astype(jnp.bfloat16), values[0:stop, :], preferred_element_type=jnp.float32
        )
        context = (weighted / total).astype(jnp.bfloat16)
        for piece in range(per_row):
            out_ref[piece, row] = context[piece * part : (piece + 1) * part]


def attention(marks, query, key, value, inverse):
    slots, part, _ = query.shape
    length = slots * part
    half = HD // 2
    freqs = jnp.exp(-math.log(10000.0) * 2.0 * jnp.arange(half, dtype=jnp.float32) / HD)
    angles = jnp.arange(length, dtype=jnp.int32).astype(jnp.float32)[:, None] * freqs[None, :]
    cosine = jnp.cos(angles)
    sine = jnp.sin(angles)
    whole = pl.BlockSpec(memory_space=pltpu.VMEM)
    return pl.pallas_call(
        attention_kernel,
        out_shape=jax.ShapeDtypeStruct((4, slots // 4, part, HD), jnp.bfloat16),
        in_specs=[pl.BlockSpec(memory_space=pltpu.SMEM)] + [whole] * 6,
        out_specs=whole,
        scratch_shapes=[pltpu.VMEM((length, HD), jnp.bfloat16)] * 3,
        compiler_params=pltpu.CompilerParams(vmem_limit_bytes=48 * 1024 * 1024),
        cost_estimate=pl.CostEstimate(
            flops=2 * length * length * HD,
            bytes_accessed=16 * length * HD,
            transcendentals=length * length // 2,
        ),
    )(
        marks,
        query,
        key,
        value,
        inverse,
        jnp.concatenate((cosine, cosine), axis=1),
        jnp.concatenate((-sine, sine), axis=1),
    )


def local_call(kernel, outputs, operands, flops=0, scratch=()):
    whole = pl.BlockSpec(memory_space=pltpu.VMEM)
    moved = sum(x.size * x.dtype.itemsize for x in (*operands, *outputs))
    return pl.pallas_call(
        kernel,
        out_shape=tuple(outputs),
        in_specs=[pl.BlockSpec(memory_space=pltpu.SMEM)] + [whole] * (len(operands) - 1),
        out_specs=(whole,) * len(outputs),
        scratch_shapes=list(scratch),
        compiler_params=pltpu.CompilerParams(vmem_limit_bytes=48 * 1024 * 1024),
        cost_estimate=pl.CostEstimate(flops=flops, bytes_accessed=moved, transcendentals=0),
    )(*operands)


def shape(like, *dims):
    return jax.ShapeDtypeStruct(dims, like.dtype)


def span(index, size):
    return pl.ds(pl.multiple_of(index * size, size), size)


def corners_kernel(marks, hidden_ref, gain_ref, own, along_y, along_x, along_xy):
    x, y = marks[X], marks[Y]
    rows, width = own.shape
    for out, h, side in ((along_y, x, 1 - y), (along_x, 1 - x, y), (along_xy, 1 - x, 1 - y), (own, x, y)):
        block = hidden_ref[span(h, rows), span(side, width)].astype(jnp.float32)
        gain = gain_ref[:, span(side, width)].astype(jnp.float32)
        out[...] = (block * gain).astype(out.dtype)


def arrange_kernel(marks, v_ref, k_ref, q_ref, vk_keep, vk_send, q_keep, q_send):
    zh, zl, y = marks[ZH], marks[ZL], marks[Y]

    def head(high, middle, low):
        return span(high * 4 + middle * 2 + low, HD)

    for middle, vk_out, q_out in ((1 - zl, vk_send, q_send), (zl, vk_keep, q_keep)):
        for i, high in enumerate((1 - y, y)):
            for j, low in enumerate((1 - zh, zh)):
                at = (i * 2 + j) * 2
                vk_out[:, at * HD : (at + 1) * HD] = v_ref[:, head(high, middle, low)]
                vk_out[:, (at + 1) * HD : (at + 2) * HD] = k_ref[:, head(high, middle, low)]
                at = i * 2 + j
                q_out[:, at * HD : (at + 1) * HD] = q_ref[:, head(high, middle, low)]


def arrange_out_kernel(marks, w_ref, keep, send):
    zh, zl = marks[ZH], marks[ZL]
    width = keep.shape[1]
    for out, mine in ((send, 1 - zl), (keep, zl)):
        for i in range(2):
            for j in range(2):
                at = i * 2 + j
                out[at * HD : (at + 1) * HD, :] = w_ref[
                    span(2 * (i ^ mine) + (j ^ zh), HD), span(mine, width)
                ]


def project_kernel(marks, *refs):
    keep_ref, got_ref, send_out, keep_out = refs[-4:]
    inputs = refs[:-4]
    middle = keep_ref.shape[1] // 2

    def run(first, second):
        for i in range(0, len(inputs), 2):
            rows = inputs[i].shape[0]
            at = pl.ds(i // 2 * rows, rows)
            for out, columns in ((send_out, pl.ds(0, middle)), (keep_out, pl.ds(middle, middle))):
                out[at, :] = (
                    jnp.dot(inputs[i][...], first[:, columns], preferred_element_type=jnp.float32)
                    + jnp.dot(
                        inputs[i + 1][...], second[:, columns], preferred_element_type=jnp.float32
                    )
                ).astype(out.dtype)

    @pl.when(marks[ZL] == marks[CORE])
    def _():
        run(keep_ref, got_ref)

    @pl.when(marks[ZL] != marks[CORE])
    def _():
        run(got_ref, keep_ref)


def project(marks, pairs, keep, got):
    inputs = [block for pair in pairs for block in pair]
    rows = sum(pair[0].shape[0] for pair in pairs)
    depth, columns = keep.shape
    outputs = (
        jax.ShapeDtypeStruct((rows, columns // 2), jnp.bfloat16),
        jax.ShapeDtypeStruct((rows, columns // 2), jnp.float32),
    )
    return local_call(
        project_kernel, outputs, (marks, *inputs, keep, got), flops=4 * rows * depth * columns
    )


def out_kernel(marks, own_ref, other_ref, keep_ref, got_ref, send_0, send_1, keep_0, keep_1, joined):
    part = own_ref.shape[-2]
    depth = keep_ref.shape[0]
    aside = marks[ZL] ^ marks[CORE]
    for first in range(8):
        order = ((first & 3) << 1) | (first >> 2)
        row = (order ^ 7) ^ (marks[ZH] * 4 + marks[ZL] * 2 + marks[Y])
        for h in range(2):
            at = pl.ds((first * 2 + h) * part, part)
            for ref, place in ((own_ref, aside), (other_ref, 1 - aside)):
                for block in range(4):
                    joined[at, span(place * 4 + block, HD)] = ref[h, block >> 1, block & 1, row]
    rows, columns = send_0.shape
    for at, outs in ((0, (send_0, send_1)), (rows, (keep_0, keep_1))):
        for side, out in enumerate(outs):
            across = pl.ds(side * columns, columns)
            out[...] = (
                jnp.dot(
                    joined[at : at + rows, :depth],
                    keep_ref[:, across],
                    preferred_element_type=jnp.float32,
                )
                + jnp.dot(
                    joined[at : at + rows, depth:],
                    got_ref[:, across],
                    preferred_element_type=jnp.float32,
                )
            ).astype(out.dtype)


def home_kernel(marks, *refs):
    out_ref = refs[-1]
    here = marks[ZH] * 4 + marks[ZL] * 2 + marks[Y]
    for mask, ref in enumerate(refs[:-1]):
        peer = here ^ mask
        head = ((peer & 1) << 2) | (peer & 2) | (peer >> 2)
        out_ref[:, span(head, HD)] = ref[...]


def finish_kernel(marks, hidden_ref, *refs):
    out_ref = refs[-1]
    rows, width = refs[0].shape
    part = rows // 2
    for j in range(2):
        for place, ref in ((marks[ZL], refs[2 * j]), (1 - marks[ZL], refs[2 * j + 1])):
            for h in range(2):
                at = span((h ^ marks[X]) * 2 + j, part)
                block = hidden_ref[at, span(place, width)].astype(jnp.float32)
                added = ref[h * part : (h + 1) * part, :].astype(jnp.float32)
                out_ref[at, span(place, width)] = (block + added).astype(out_ref.dtype)


def after(values, *earlier):
    return lax.optimization_barrier((values, *earlier))[0]


def on_device_paired(hidden, norm_gain, w_query, w_key, w_value, w_out):
    rows, cols = lax.axis_size("row"), lax.axis_size("col")
    tokens, width = hidden.shape[0], hidden.shape[1] // 2
    length = tokens * rows
    row, col = lax.axis_index("row"), lax.axis_index("col")
    y, zl, zh = row & 1, (row >> 1) & 1, row >> 2
    core, x = col & 1, col >> 1
    marks = jnp.stack((x, core, zh, zl, y)).astype(jnp.int32)
    steps = {"y": (1, 0), "zl": (2, 0), "zh": (4, 0), "core": (0, 1), "x": (0, 2), "xy": (1, 2)}

    def swap(values, name):
        by_row, by_col = steps[name]
        pairs = [
            (r * cols + c, (r ^ by_row) * cols + (c ^ by_col))
            for r in range(rows)
            for c in range(cols)
        ]
        return lax.ppermute(values, ("row", "col"), pairs)

    def ordered(mine, other, bit):
        return jnp.where(bit == 0, mine, other), jnp.where(bit == 0, other, mine)

    part = tokens // 2
    small = part // 2
    quarter = shape(hidden, part, width)
    own, to_y, to_x, to_xy = local_call(
        corners_kernel, (quarter,) * 4, (marks, hidden, norm_gain.reshape(1, -1))
    )
    from_xy, from_x, from_y = swap(to_xy, "xy"), swap(to_x, "x"), swap(to_y, "y")

    depth = w_value.shape[0]
    double, single = shape(w_value, depth, 8 * HD), shape(w_value, depth, 4 * HD)
    vk_keep, vk_send, q_keep, q_send = local_call(
        arrange_kernel,
        (double, double, single, single),
        (after(marks, own), w_value, w_key, w_query),
    )
    vk_got = swap(vk_send, "zl")

    mine = jnp.stack(ordered(own, from_y, y))
    theirs = jnp.stack(ordered(from_x, from_xy, y))
    block, send = ordered(mine, theirs, x ^ zh)
    landed = [block, swap(send, "zh")]

    inputs = []
    for block in landed:
        for j in range(2):
            held = block[:, j * small : (j + 1) * small].reshape(2 * small, width)
            held = jnp.concatenate((held, swap(held, "zl")), axis=0)
            held = jnp.concatenate((held, swap(held, "x")), axis=0)
            inputs.append((held, swap(held, "core")))
    q_got = swap(after(q_send, vk_got, inputs[1][0]), "zl")

    def halves(values, axis=1):
        middle = values.shape[axis] // 2
        return jnp.split(values, [middle], axis=axis)

    units = [((pair,), vk_keep, vk_got) for pair in inputs]
    units += [(two, q_keep, q_got) for two in (inputs[:2], inputs[2:])]
    sums, kept, got = [], [], []
    for i, (pairs, first, second) in enumerate(units):
        send, keep = project(marks, pairs, first, second)
        if i >= 2:
            send = after(send, sums[i - 2])
        if i >= 4:
            send = after(send, got[i - 4])
        total = keep + swap(send, "y").astype(jnp.float32)
        send, keep = halves(total)
        sums.append(send.astype(jnp.bfloat16))
        kept.append(keep)
        got.append(swap(sums[-1], "zh").astype(jnp.float32))
    results = [kept[i] + got[p] for i, p in enumerate((2, 3, 0, 1, 5, 4))]

    residual = after(hidden, sums[0]).astype(jnp.float32)
    squares = jnp.sum(residual * residual, axis=1).reshape(1, tokens)
    squares = squares + swap(squares, "core")
    squares = squares + swap(squares, "x")
    for name, bit in (("y", y), ("zl", zl), ("zh", zh)):
        squares = jnp.concatenate(ordered(squares, swap(squares, name), bit), axis=0)
    mean = squares / (hidden.shape[1] * cols)
    inverse = lax.rsqrt(mean + norm_epsilon).reshape(length, 1)

    both = jnp.concatenate(results[:4], axis=0)
    query = jnp.concatenate(results[4:], axis=0).reshape(-1, small, HD)
    value = both[:, :HD].reshape(-1, small, HD)
    key = both[:, HD:].reshape(-1, small, HD)
    context = attention(marks, query, key, value, inverse)

    out_depth, out_width = w_out.shape
    half = shape(w_out, out_depth, out_width // 2)
    out_keep, out_send = local_call(arrange_out_kernel, (half, half), (after(marks, q_send), w_out))
    out_got = swap(after(out_send, q_got), "zl")

    gathered, crossed = [], []
    for j in range(2):
        held = lax.dynamic_index_in_dim(context, x * 2 + j, 0, keepdims=False)
        send = lax.dynamic_index_in_dim(context, (1 - x) * 2 + j, 0, keepdims=False)
        held, send = ordered(held, swap(send, "x"), x ^ zh)
        crossed.append(swap(send, "zh"))
        held = jnp.stack((held, crossed[-1]))
        held = jnp.stack((held, swap(held, "zl")))
        held = jnp.stack((held, swap(held, "x")))
        gathered.append((held, swap(held, "core")))

    blocks = []
    for mask in range(rows):
        block = lax.dynamic_index_in_dim(context, row ^ mask, 1, keepdims=False)
        if mask:
            pairs = [(i, i ^ mask) for i in range(rows)]
            block = lax.ppermute(after(block, crossed[1]), "row", pairs)
        blocks.append(block.reshape(tokens, HD))
    (context_out,) = local_call(
        home_kernel, (shape(hidden, tokens, rows * HD),), (marks, *blocks)
    )

    sums, finals = [], []
    for held in gathered:
        count = rows * small
        outputs = (jax.ShapeDtypeStruct((count, out_width // 4), jnp.bfloat16),) * 2
        outputs += (jax.ShapeDtypeStruct((count, out_width // 4), jnp.float32),) * 2
        products = local_call(
            out_kernel,
            outputs,
            (marks, *held, out_keep, out_got),
            flops=8 * count * out_depth * out_width,
            scratch=[pltpu.VMEM((2 * count, 2 * out_depth), jnp.bfloat16)],
        )
        mine, theirs = [], []
        for send, keep in zip(products[:2], products[2:]):
            if len(sums) >= 2:
                send = after(send, sums[-2])
            total = keep + swap(send, "y").astype(jnp.float32)
            send, keep = halves(total, 0)
            sums.append(send.astype(jnp.bfloat16))
            total = keep + swap(sums[-1], "zh").astype(jnp.float32)
            send, keep = halves(total.astype(jnp.bfloat16), 0)
            theirs.append(send)
            mine.append(keep)
        finals.append(jnp.concatenate(mine, axis=1))
        finals.append(swap(jnp.concatenate(theirs, axis=1), "zl"))

    (layer_out,) = local_call(
        finish_kernel, (shape(hidden, *hidden.shape),), (marks, hidden, *finals)
    )
    return (context_out, layer_out)


def on_device(hidden, norm_gain, w_query, w_key, w_value, w_out):
    rows, cols = lax.axis_size("row"), lax.axis_size("col")
    heads_here = w_query.shape[1] // HD
    paired = rows == 2**3 and cols == 2**2 and heads_here == rows and hidden.shape[0] % 64 == 0
    plan = on_device_paired if paired else on_device_any
    return plan(hidden, norm_gain, w_query, w_key, w_value, w_out)


def solution(mesh):
    placed = (
        P("row", "col"),
        P("col"),
        P("row", "col"),
        P("row", "col"),
        P("row", "col"),
        P("row", "col"),
    )
    return jax.shard_map(
        on_device,
        mesh=mesh,
        in_specs=placed,
        out_specs=(P("row", "col"), P("row", "col")),
        check_vma=False,
    )
```

```python
import functools
import math

import jax
import jax.numpy as jnp
from jax import lax
from jax.experimental import pallas as pl
from jax.experimental.pallas import tpu as pltpu
from jax.sharding import PartitionSpec as P

HD = 128


norm_epsilon = 1e-05

X, CORE, ZH, ZL, Y = range(5)


def rotary(values, positions):
    half = values.shape[-1] // 2
    freqs = jnp.exp(
        -math.log(10000.0) * 2.0 * jnp.arange(half, dtype=jnp.float32) / values.shape[-1]
    )
    angles = positions.astype(jnp.float32)[:, None] * freqs[None, :]
    cosine = jnp.cos(angles)[:, None, :]
    sine = jnp.sin(angles)[:, None, :]
    first = values[..., :half]
    second = values[..., half:]
    return jnp.concatenate(
        (first * cosine - second * sine, second * cosine + first * sine), axis=-1
    )


def attend(carry, keys, values, queries, query_positions, key_positions, scale):
    peak, total, weighted = carry
    scores = jnp.einsum("qhd,khd->hqk", queries, keys, preferred_element_type=jnp.float32) * scale
    allowed = key_positions[None, :] <= query_positions[:, None]
    scores = jnp.where(allowed[None, :, :], scores, -jnp.inf)
    new_peak = jnp.maximum(peak, jnp.max(scores, axis=2))
    probs = jnp.exp(scores - new_peak[:, :, None])
    total = jnp.sum(probs, axis=2)
    weighted = jnp.einsum(
        "hqk,khd->hqd", probs.astype(jnp.bfloat16), values, preferred_element_type=jnp.float32
    )
    return (new_peak, total, weighted)


def start_state(heads_here, count):
    return (
        jnp.full((heads_here, count), -1e30, jnp.float32),
        jnp.zeros((heads_here, count), jnp.float32),
        jnp.zeros((heads_here, count, HD), jnp.float32),
    )


def finish(carry, count, heads_here):
    peak, total, weighted = carry
    return (
        (weighted / total[:, :, None])
        .transpose(1, 0, 2)
        .reshape(count, heads_here * HD)
        .astype(jnp.bfloat16)
    )


def on_device_any(hidden, norm_gain, w_query, w_key, w_value, w_out):
    rows = hidden.shape[0]
    features = hidden.shape[1] * lax.axis_size("col")
    residual = hidden.astype(jnp.float32)
    squares = lax.psum(jnp.sum(residual * residual, axis=1), "col")
    scaled = (
        residual
        * lax.rsqrt(squares / features + norm_epsilon)[:, None]
        * norm_gain.astype(jnp.float32)[None, :]
    )
    normed = lax.all_gather(scaled.astype(jnp.bfloat16), "col", axis=1, tiled=True)
    spread = lax.all_to_all(normed, "row", split_axis=1, concat_axis=0, tiled=True)
    joined = jnp.concatenate((w_query, w_key, w_value), axis=1)
    summed = lax.psum_scatter(
        jnp.dot(spread, joined, preferred_element_type=jnp.float32).astype(jnp.bfloat16),
        "row",
        scatter_dimension=0,
        tiled=True,
    ).astype(jnp.float32)
    proj_q, proj_k, proj_v = jnp.split(summed, 3, axis=1)
    heads_here = w_query.shape[1] // HD
    row_index = lax.axis_index("row")
    first_row = row_index * rows
    positions = first_row + jnp.arange(rows, dtype=jnp.int32)
    query = rotary(proj_q.reshape(rows, heads_here, HD), positions).astype(jnp.bfloat16)
    keys_here = (
        rotary(proj_k.reshape(rows, heads_here, HD), positions)
        .astype(jnp.bfloat16)
        .reshape(rows, heads_here * HD)
    )
    values_here = proj_v.astype(jnp.bfloat16)
    scale = 1.0 / math.sqrt(HD)
    initial = start_state(heads_here, rows)
    keys = lax.all_gather(keys_here, "row", axis=0, tiled=True).reshape(-1, heads_here, HD)
    values = lax.all_gather(values_here, "row", axis=0, tiled=True).reshape(-1, heads_here, HD)
    key_positions = jnp.arange(keys.shape[0], dtype=jnp.int32)
    folded = attend(initial, keys, values, query, positions, key_positions, scale)
    context = finish(folded, rows, heads_here)
    gathered_context = lax.all_gather(context, "col", axis=1, tiled=True)
    spread_context = lax.all_to_all(
        gathered_context, "row", split_axis=1, concat_axis=0, tiled=True
    )
    attended = lax.psum_scatter(
        jnp.dot(spread_context, w_out, preferred_element_type=jnp.float32).astype(jnp.bfloat16),
        "row",
        scatter_dimension=0,
        tiled=True,
    ).astype(jnp.float32)
    layer_out = (residual + attended).astype(jnp.bfloat16)
    return (context, layer_out)


def attention_kernel(marks, q_ref, k_ref, v_ref, cos_ref, sin_ref, out_ref, query, keys, values):
    half = HD // 2
    slots, part = q_ref.shape[0], q_ref.shape[1]
    block = part * 2
    pieces = out_ref.shape[0]
    small = block // pieces
    factor = math.log2(math.e) / math.sqrt(HD)

    def turned(raw, at):
        return (raw * cos_ref[at, :] + pltpu.roll(raw, half, 1) * sin_ref[at, :]).astype(
            jnp.bfloat16
        )

    for row in range(slots // 2):
        zh, zl, y = row >> 2, (row >> 1) & 1, row & 1
        for h in range(2):
            slot = (zh ^ marks[ZH]) * 2 + (h ^ marks[X])
            slot = (slot * 2 + (zl ^ marks[ZL])) * 2 + y
            at = pl.ds(row * block + h * part, part)
            query[at, :] = turned(q_ref[slot], at)
            keys[at, :] = turned(k_ref[slot], at)
            values[at, :] = v_ref[slot].astype(jnp.bfloat16)
        start, stop = row * block, (row + 1) * block
        scores = lax.dot_general(
            query[start:stop, :],
            keys[0:stop, :],
            (((1,), (1,)), ((), ())),
            preferred_element_type=jnp.float32,
        )
        down = lax.broadcasted_iota(jnp.int32, scores.shape, 0) + start
        along = lax.broadcasted_iota(jnp.int32, scores.shape, 1)
        scores = jnp.where(along <= down, scores, -jnp.inf)
        peak = jnp.max(scores, axis=1, keepdims=True)
        probs = jnp.exp2((scores - peak) * factor)
        total = jnp.sum(probs, axis=1, keepdims=True)
        weighted = jnp.dot(
            probs.astype(jnp.bfloat16), values[0:stop, :], preferred_element_type=jnp.float32
        )
        context = (weighted / total).astype(jnp.bfloat16)
        for piece in range(pieces):
            out_ref[piece, row] = context[piece * small : (piece + 1) * small]


def turning(positions):
    half = HD // 2
    freqs = jnp.exp(-math.log(10000.0) * 2.0 * jnp.arange(half, dtype=jnp.float32) / HD)
    angles = positions.astype(jnp.float32)[:, None] * freqs[None, :]
    cosine = jnp.cos(angles)
    sine = jnp.sin(angles)
    return jnp.concatenate((cosine, cosine), axis=1), jnp.concatenate((-sine, sine), axis=1)


def attention(marks, query, key, value, cosine, sine):
    slots, part, _ = query.shape
    length = slots * part
    (context,) = local_call(
        attention_kernel,
        (jax.ShapeDtypeStruct((4, slots // 2, part // 2, HD), jnp.bfloat16),),
        (marks, query, key, value, cosine, sine),
        scratch=[jax.ShapeDtypeStruct((length, HD), jnp.bfloat16)] * 3,
        spare=12,
    )
    return context


def local_call(kernel, outputs, operands, scratch=(), spare=4):
    whole = pl.BlockSpec(memory_space=pltpu.VMEM)
    needed = sum(max(x.size, 1024) * x.dtype.itemsize for x in (*operands, *outputs, *scratch))
    return pl.pallas_call(
        kernel,
        name=getattr(kernel, "__name__", "corners_kernel"),
        out_shape=tuple(outputs),
        in_specs=[pl.BlockSpec(memory_space=pltpu.SMEM)] + [whole] * (len(operands) - 1),
        out_specs=(whole,) * len(outputs),
        scratch_shapes=[pltpu.VMEM(x.shape, x.dtype) for x in scratch],
        compiler_params=pltpu.CompilerParams(vmem_limit_bytes=needed + spare * 1024 * 1024),
        cost_estimate=pl.CostEstimate(flops=1, bytes_accessed=1, transcendentals=0),
    )(*operands)


def shape(like, *dims):
    return jax.ShapeDtypeStruct(dims, like.dtype)


def span(index, size):
    return pl.ds(pl.multiple_of(index * size, size), size)


def squares_kernel(marks, hidden_ref, out_ref):
    values = hidden_ref[...].astype(jnp.float32)
    total = jnp.sum(values * values, axis=1, keepdims=True)
    out_ref[...] = jnp.broadcast_to(total, out_ref.shape)


def corners_kernel(features, marks, hidden_ref, gain_ref, sum_0, sum_1, along_xy, along_x, along_y, own):
    x, y = marks[X], marks[Y]
    rows, width = own.shape
    places = ((1 - x, 1 - y), (1 - x, y), (x, 1 - y), (x, y))
    for out, (h, side) in zip((along_xy, along_x, along_y, own), places):
        block = hidden_ref[span(h, rows), span(side, width)].astype(jnp.float32)
        gain = gain_ref[:, span(side, width)].astype(jnp.float32)
        mean = (sum_0[span(h, rows), 0:1] + sum_1[span(h, rows), 0:1]) / features
        out[...] = (block * lax.rsqrt(mean + norm_epsilon) * gain).astype(out.dtype)


def arrange_kernel(marks, w_ref, keep, send):
    zh, zl, y = marks[ZH], marks[ZL], marks[Y]
    for middle, out in ((1 - zl, send), (zl, keep)):
        for i, high in enumerate((1 - y, y)):
            for j, low in enumerate((1 - zh, zh)):
                at = (i * 2 + j) * HD
                out[:, at : at + HD] = w_ref[:, span(high * 4 + middle * 2 + low, HD)]


def arrange_out_kernel(marks, w_ref, keep, send):
    zh, zl = marks[ZH], marks[ZL]
    width = keep.shape[1]
    for out, mine in ((send, 1 - zl), (keep, zl)):
        for i in range(2):
            for j in range(2):
                at = i * 2 + j
                out[at * HD : (at + 1) * HD, :] = w_ref[
                    span(2 * (i ^ mine) + (j ^ zh), HD), span(mine, width)
                ]


def project_kernel(marks, *refs):
    first, second, send_out, keep_out = refs[-4:]
    inputs = refs[:-4]
    middle = first.shape[1] // 2
    for i in range(0, len(inputs), 2):
        rows = inputs[i].shape[0]
        into = pl.ds(i // 2 * rows, rows)
        for out, columns in ((send_out, pl.ds(0, middle)), (keep_out, pl.ds(middle, middle))):
            out[into, :] = (
                jnp.dot(inputs[i][...], first[:, columns], preferred_element_type=jnp.float32)
                + jnp.dot(
                    inputs[i + 1][...], second[:, columns], preferred_element_type=jnp.float32
                )
            ).astype(out.dtype)


def project(marks, pairs, first, second):
    inputs = [block for pair in pairs for block in pair]
    rows = sum(pair[0].shape[0] for pair in pairs)
    columns = first.shape[1]
    outputs = (
        jax.ShapeDtypeStruct((rows, columns // 2), jnp.bfloat16),
        jax.ShapeDtypeStruct((rows, columns // 2), jnp.float32),
    )
    return local_call(project_kernel, outputs, (marks, *inputs, first, second))


def out_kernel(
    marks, own_0, own_1, other_0, other_1, keep_ref, got_ref, send_0, send_1, keep_0, keep_1, joined
):
    part = own_0.shape[-2]
    depth = keep_ref.shape[0]
    aside = marks[ZL] ^ marks[CORE]
    for first in range(8):
        order = ((first & 3) << 1) | (first >> 2)
        row = (order ^ 7) ^ (marks[ZH] * 4 + marks[ZL] * 2 + marks[Y])
        for h, (own, other) in enumerate(((own_0, other_0), (own_1, other_1))):
            at = pl.ds((first * 2 + h) * part, part)
            for ref, place in ((own, aside), (other, 1 - aside)):
                for block in range(4):
                    joined[at, span(place * 4 + block, HD)] = ref[block >> 1, block & 1, row]
    rows, columns = send_0.shape
    for at, outs in ((0, (send_0, send_1)), (rows, (keep_0, keep_1))):
        for side, out in enumerate(outs):
            across = pl.ds(side * columns, columns)
            out[...] = (
                jnp.dot(
                    joined[at : at + rows, :depth],
                    keep_ref[:, across],
                    preferred_element_type=jnp.float32,
                )
                + jnp.dot(
                    joined[at : at + rows, depth:],
                    got_ref[:, across],
                    preferred_element_type=jnp.float32,
                )
            ).astype(out.dtype)


def home_kernel(marks, keep_ref, got_ref, out_ref):
    pieces, small = keep_ref.shape[2:4]
    for aside, ref in enumerate((keep_ref, got_ref)):
        for block in range(4):
            zl, zh = block >> 1, block & 1
            head = (marks[Y] ^ aside) * 4 + (marks[ZL] ^ zl) * 2 + (marks[ZH] ^ zh)
            for piece in range(pieces):
                out_ref[piece * small : (piece + 1) * small, span(head, HD)] = ref[zl, zh, piece]


def finish_kernel(marks, hidden_ref, *refs):
    out_ref = refs[-1]
    rows, width = refs[0].shape
    part = rows // 2
    for j in range(2):
        for place, ref in ((marks[ZL], refs[2 * j]), (1 - marks[ZL], refs[2 * j + 1])):
            for h in range(2):
                at = span((h ^ marks[X]) * 2 + j, part)
                block = hidden_ref[at, span(place, width)].astype(jnp.float32)
                added = ref[h * part : (h + 1) * part, :].astype(jnp.float32)
                out_ref[at, span(place, width)] = (block + added).astype(out_ref.dtype)


def after(values, *earlier):
    return lax.optimization_barrier((values, *earlier))[0]


def on_device_paired(hidden, norm_gain, w_query, w_key, w_value, w_out):
    rows, cols = lax.axis_size("row"), lax.axis_size("col")
    tokens, width = hidden.shape[0], hidden.shape[1] // 2
    length = tokens * rows
    row, col = lax.axis_index("row"), lax.axis_index("col")
    y, zl, zh = row & 1, (row >> 1) & 1, row >> 2
    core, x = col & 1, col >> 1
    marks = jnp.stack((x, core, zh, zl, y)).astype(jnp.int32)
    steps = {"y": (1, 0), "zl": (2, 0), "zh": (4, 0), "core": (0, 1), "x": (0, 2), "xy": (1, 2)}

    def swap(values, name):
        by_row, by_col = steps[name]
        pairs = [
            (r * cols + c, (r ^ by_row) * cols + (c ^ by_col))
            for r in range(rows)
            for c in range(cols)
        ]
        return lax.ppermute(values, ("row", "col"), pairs)

    def spread(block, along, *earlier):
        held = jnp.concatenate((block, along))
        beside = swap(after(held, *earlier), "x")
        return held, swap(held, "core"), beside

    def ordered(mine, other, bit):
        return jnp.where(bit == 0, mine, other), jnp.where(bit == 0, other, mine)

    def index(values, at, axis=0):
        return lax.dynamic_index_in_dim(values, at, axis, keepdims=False)

    def halves(values):
        middle = values.shape[0] // 2
        return values[:middle], values[middle:]

    sums_shape = jax.ShapeDtypeStruct((tokens, HD), jnp.float32)
    (squares,) = local_call(squares_kernel, (sums_shape,), (marks, hidden))
    depth = w_value.shape[0]

    def arranged(weight, *earlier):
        half = shape(weight, depth, 4 * HD)
        return local_call(arrange_kernel, (half, half), (after(marks, *earlier), weight))

    v_keep, v_send = arranged(w_value)
    v_got = swap(v_send, "zl")
    squares = squares + swap(squares, "core")
    squares = after(squares, v_send)
    squares_x = swap(squares, "x")

    quarter = shape(hidden, tokens // 2, width)
    to_xy, to_x, to_y, own = local_call(
        functools.partial(corners_kernel, hidden.shape[1] * cols),
        (quarter,) * 4,
        (marks, hidden, norm_gain.reshape(1, -1), squares, squares_x),
    )
    from_xy, from_x, from_y = swap(to_xy, "xy"), swap(to_x, "x"), swap(to_y, "y")

    mine = jnp.concatenate(ordered(own, from_y, y))
    theirs = jnp.concatenate(ordered(from_x, from_xy, y))
    block_a, send = ordered(mine, theirs, x ^ zh)
    along_a = swap(after(block_a, v_got), "zl")
    block_b = swap(after(send, along_a), "zh")

    k_keep, k_send = arranged(w_key, to_y)
    q_keep, q_send = arranged(w_query, to_y)
    positions = jnp.arange(length, dtype=jnp.int32)
    cosine, sine = turning(after(positions, to_y))
    out_depth, out_width = w_out.shape
    half = shape(w_out, out_depth, out_width // 2)
    out_keep, out_send = local_call(arrange_out_kernel, (half, half), (after(marks, to_y), w_out))

    along_a = after(along_a, k_send, q_send, cosine, sine, out_send)
    k_got = swap(after(k_send, along_a), "zl")
    held_a, core_a, beside_a = spread(block_a, along_a)
    pairs_a = ((held_a, core_a), (beside_a, swap(beside_a, "core")))
    along_b = swap(block_b, "zl")
    held_b, core_b, beside_b = spread(block_b, along_b, beside_a)
    q_got = swap(after(q_send, k_got), "zl")

    def multiply(pairs, keep, got, *earlier):
        return project(after(marks, *earlier), pairs, *ordered(keep, got, zl ^ core))

    weights = ((v_keep, v_got), (k_keep, k_got), (q_keep, q_got))
    products = [multiply(pairs_a, *weights[0])]
    products.append(multiply(pairs_a, *weights[1], products[0][0]))
    sums, kept, got = [], [], []
    for i in range(6):
        if i == 1:
            products.append(multiply(pairs_a, *weights[2], sums[0]))
            beside_b = after(beside_b, sums[0])
            pairs_b = ((held_b, core_b), (beside_b, swap(beside_b, "core")))
        if 2 <= i < 5:
            products.append(multiply(pairs_b, *weights[i - 2], sums[i - 1]))
        send, keep = products[i]
        if i >= 2:
            send = after(send, sums[i - 2])
            keep = after(keep, got[i - 2])
        if i < 5:
            keep = after(keep, products[i + 1][0])
        total = keep + swap(send, "y").astype(jnp.float32)
        sums.append(total[:, :HD].astype(jnp.bfloat16))
        kept.append(total[:, HD:])
        got.append(swap(sums[-1], "zh"))

    value, key, query = (
        jnp.concatenate((kept[a] + got[b].astype(jnp.float32), kept[b] + got[a].astype(jnp.float32)))
        .reshape(-1, tokens // 2, HD)
        for a, b in ((0, 3), (1, 4), (2, 5))
    )
    context = attention(marks, query, key, value, cosine, sine)
    pieces, _, small, _ = context.shape

    out_got = swap(after(out_send, q_got), "zl")
    context = after(context, out_got)

    sides = context.reshape(2, pieces // 2, rows, small, HD)
    outward = index(sides, 1 - x)
    held, crossed = [], []
    for j in range(pieces // 2):
        near, send = ordered(index(sides, x)[j], swap(outward[j], "x"), x ^ zh)
        held.append(near)
        crossed.append(swap(send, "zh"))
    blocks = [jnp.stack((held[j], crossed[j])) for j in range(pieces // 2)]
    alongs = [swap(block, "zl") for block in blocks]
    sums, got, mine, theirs, finals = [], [], [], [], []
    count = rows * small
    outputs = (jax.ShapeDtypeStruct((count, out_width // 4), jnp.bfloat16),) * 2
    outputs += (jax.ShapeDtypeStruct((count, out_width // 4), jnp.float32),) * 2
    products = []
    for block, along in zip(blocks, alongs):
        block = jnp.stack((block, along))
        beside = swap(block, "x")
        further = swap(after(beside, alongs[-1], *(sent[0] for sent in products)), "core")
        products.append(
            local_call(
                out_kernel,
                outputs,
                (marks, block, beside, swap(block, "core"), further, out_keep, out_got),
                scratch=[jax.ShapeDtypeStruct((2 * count, 2 * out_depth), jnp.bfloat16)],
            )
        )
    first, second = products
    block = after(context, first[0]).reshape(pieces, 2, 2, 2, small, HD)
    home = jnp.stack((index(block, zh, 1), swap(index(block, 1 - zh, 1), "zh")))
    for i, (send, keep) in enumerate(
        ((first[0], first[2]), (first[1], first[3]), (second[0], second[2]), (second[1], second[3]))
    ):
        if i == 0:
            keep = after(keep, home)
        if i == 3:
            home = jnp.stack((index(home, zl, 2), swap(index(home, 1 - zl, 2), "zl")))
            keep = after(keep, home)
        if i >= 2:
            send = after(send, sums[i - 2])
        if i >= 3:
            send = after(send, got[i - 3])
        total = keep + swap(send, "y").astype(jnp.float32)
        send, keep = halves(total)
        sums.append(send.astype(jnp.bfloat16))
        got.append(swap(sums[-1], "zh"))
        send, keep = halves((keep + got[-1].astype(jnp.float32)).astype(jnp.bfloat16))
        theirs.append(send)
        mine.append(keep)
        if i & 1:
            finals.append(jnp.concatenate(mine[-2:], axis=1))
            finals.append(swap(jnp.concatenate(theirs[-2:], axis=1), "zl"))

    home = after(home, sums[3])
    (context_out,) = local_call(
        home_kernel,
        (shape(hidden, tokens, rows * HD),),
        (marks, index(home, y, 3), swap(index(home, 1 - y, 3), "y")),
    )
    (layer_out,) = local_call(
        finish_kernel, (shape(hidden, *hidden.shape),), (marks, hidden, *finals)
    )
    return (context_out, layer_out)


def on_device(hidden, norm_gain, w_query, w_key, w_value, w_out):
    rows, cols = lax.axis_size("row"), lax.axis_size("col")
    heads_here = w_query.shape[1] // HD
    paired = rows == 2**3 and cols == 2**2 and heads_here == rows and hidden.shape[0] % 64 == 0
    plan = on_device_paired if paired else on_device_any
    return plan(hidden, norm_gain, w_query, w_key, w_value, w_out)


def solution(mesh):
    placed = (
        P("row", "col"),
        P("col"),
        P("row", "col"),
        P("row", "col"),
        P("row", "col"),
        P("row", "col"),
    )
    return jax.shard_map(
        on_device,
        mesh=mesh,
        in_specs=placed,
        out_specs=(P("row", "col"), P("row", "col")),
        check_vma=False,
    )
```

```python
import functools
import math

import jax
import jax.numpy as jnp
from jax import lax
from jax.experimental import pallas as pl
from jax.experimental.pallas import tpu as pltpu
from jax.sharding import PartitionSpec as P

HD = 128


norm_epsilon = 1e-05

X, CORE, ZH, ZL, Y = range(5)


def rotary(values, positions):
    half = values.shape[-1] // 2
    freqs = jnp.exp(
        -math.log(10000.0) * 2.0 * jnp.arange(half, dtype=jnp.float32) / values.shape[-1]
    )
    angles = positions.astype(jnp.float32)[:, None] * freqs[None, :]
    cosine = jnp.cos(angles)[:, None, :]
    sine = jnp.sin(angles)[:, None, :]
    first = values[..., :half]
    second = values[..., half:]
    return jnp.concatenate(
        (first * cosine - second * sine, second * cosine + first * sine), axis=-1
    )


def attend(carry, keys, values, queries, query_positions, key_positions, scale):
    peak, total, weighted = carry
    scores = jnp.einsum("qhd,khd->hqk", queries, keys, preferred_element_type=jnp.float32) * scale
    allowed = key_positions[None, :] <= query_positions[:, None]
    scores = jnp.where(allowed[None, :, :], scores, -jnp.inf)
    new_peak = jnp.maximum(peak, jnp.max(scores, axis=2))
    probs = jnp.exp(scores - new_peak[:, :, None])
    total = jnp.sum(probs, axis=2)
    weighted = jnp.einsum(
        "hqk,khd->hqd", probs.astype(jnp.bfloat16), values, preferred_element_type=jnp.float32
    )
    return (new_peak, total, weighted)


def start_state(heads_here, count):
    return (
        jnp.full((heads_here, count), -1e30, jnp.float32),
        jnp.zeros((heads_here, count), jnp.float32),
        jnp.zeros((heads_here, count, HD), jnp.float32),
    )


def finish(carry, count, heads_here):
    peak, total, weighted = carry
    return (
        (weighted / total[:, :, None])
        .transpose(1, 0, 2)
        .reshape(count, heads_here * HD)
        .astype(jnp.bfloat16)
    )


def on_device_any(hidden, norm_gain, w_query, w_key, w_value, w_out):
    rows = hidden.shape[0]
    features = hidden.shape[1] * lax.axis_size("col")
    residual = hidden.astype(jnp.float32)
    squares = lax.psum(jnp.sum(residual * residual, axis=1), "col")
    scaled = (
        residual
        * lax.rsqrt(squares / features + norm_epsilon)[:, None]
        * norm_gain.astype(jnp.float32)[None, :]
    )
    normed = lax.all_gather(scaled.astype(jnp.bfloat16), "col", axis=1, tiled=True)
    spread = lax.all_to_all(normed, "row", split_axis=1, concat_axis=0, tiled=True)
    joined = jnp.concatenate((w_query, w_key, w_value), axis=1)
    summed = lax.psum_scatter(
        jnp.dot(spread, joined, preferred_element_type=jnp.float32).astype(jnp.bfloat16),
        "row",
        scatter_dimension=0,
        tiled=True,
    ).astype(jnp.float32)
    proj_q, proj_k, proj_v = jnp.split(summed, 3, axis=1)
    heads_here = w_query.shape[1] // HD
    row_index = lax.axis_index("row")
    first_row = row_index * rows
    positions = first_row + jnp.arange(rows, dtype=jnp.int32)
    query = rotary(proj_q.reshape(rows, heads_here, HD), positions).astype(jnp.bfloat16)
    keys_here = (
        rotary(proj_k.reshape(rows, heads_here, HD), positions)
        .astype(jnp.bfloat16)
        .reshape(rows, heads_here * HD)
    )
    values_here = proj_v.astype(jnp.bfloat16)
    scale = 1.0 / math.sqrt(HD)
    initial = start_state(heads_here, rows)
    keys = lax.all_gather(keys_here, "row", axis=0, tiled=True).reshape(-1, heads_here, HD)
    values = lax.all_gather(values_here, "row", axis=0, tiled=True).reshape(-1, heads_here, HD)
    key_positions = jnp.arange(keys.shape[0], dtype=jnp.int32)
    folded = attend(initial, keys, values, query, positions, key_positions, scale)
    context = finish(folded, rows, heads_here)
    gathered_context = lax.all_gather(context, "col", axis=1, tiled=True)
    spread_context = lax.all_to_all(
        gathered_context, "row", split_axis=1, concat_axis=0, tiled=True
    )
    attended = lax.psum_scatter(
        jnp.dot(spread_context, w_out, preferred_element_type=jnp.float32).astype(jnp.bfloat16),
        "row",
        scatter_dimension=0,
        tiled=True,
    ).astype(jnp.float32)
    layer_out = (residual + attended).astype(jnp.bfloat16)
    return (context, layer_out)


def attention_kernel(marks, q_ref, k_ref, v_ref, cos_ref, sin_ref, out_ref, query, keys, values):
    half = HD // 2
    slots, part = q_ref.shape[0], q_ref.shape[1]
    block = part * 2
    pieces = out_ref.shape[0]
    small = block // pieces
    factor = math.log2(math.e) / math.sqrt(HD)

    def turned(raw, at):
        return (raw * cos_ref[at, :] + pltpu.roll(raw, half, 1) * sin_ref[at, :]).astype(
            jnp.bfloat16
        )

    for row in range(slots // 2):
        zh, zl, y = row >> 2, (row >> 1) & 1, row & 1
        for h in range(2):
            slot = (zh ^ marks[ZH]) * 2 + (h ^ marks[X])
            slot = (slot * 2 + (zl ^ marks[ZL])) * 2 + y
            at = pl.ds(row * block + h * part, part)
            query[at, :] = turned(q_ref[slot], at)
            keys[at, :] = turned(k_ref[slot], at)
            values[at, :] = v_ref[slot].astype(jnp.bfloat16)
        start, stop = row * block, (row + 1) * block
        scores = lax.dot_general(
            query[start:stop, :],
            keys[0:stop, :],
            (((1,), (1,)), ((), ())),
            preferred_element_type=jnp.float32,
        )
        down = lax.broadcasted_iota(jnp.int32, scores.shape, 0) + start
        along = lax.broadcasted_iota(jnp.int32, scores.shape, 1)
        scores = jnp.where(along <= down, scores, -jnp.inf)
        peak = jnp.max(scores, axis=1, keepdims=True)
        probs = jnp.exp2((scores - peak) * factor)
        total = jnp.sum(probs, axis=1, keepdims=True)
        weighted = jnp.dot(
            probs.astype(jnp.bfloat16), values[0:stop, :], preferred_element_type=jnp.float32
        )
        context = (weighted / total).astype(jnp.bfloat16)
        for piece in range(pieces):
            out_ref[piece, row] = context[piece * small : (piece + 1) * small]


def turning(positions):
    half = HD // 2
    freqs = jnp.exp(-math.log(10000.0) * 2.0 * jnp.arange(half, dtype=jnp.float32) / HD)
    angles = positions.astype(jnp.float32)[:, None] * freqs[None, :]
    cosine = jnp.cos(angles)
    sine = jnp.sin(angles)
    return jnp.concatenate((cosine, cosine), axis=1), jnp.concatenate((-sine, sine), axis=1)


def attention(marks, query, key, value, cosine, sine):
    slots, part, _ = query.shape
    length = slots * part
    (context,) = local_call(
        attention_kernel,
        (jax.ShapeDtypeStruct((4, slots // 2, part // 2, HD), jnp.bfloat16),),
        (marks, query, key, value, cosine, sine),
        scratch=[jax.ShapeDtypeStruct((length, HD), jnp.bfloat16)] * 3,
        spare=12,
    )
    return context


def local_call(kernel, outputs, operands, scratch=(), spare=4):
    whole = pl.BlockSpec(memory_space=pltpu.VMEM)
    needed = sum(max(x.size, 1024) * x.dtype.itemsize for x in (*operands, *outputs, *scratch))
    return pl.pallas_call(
        kernel,
        name=getattr(kernel, "__name__", "corners_kernel"),
        out_shape=tuple(outputs),
        in_specs=[pl.BlockSpec(memory_space=pltpu.SMEM)] + [whole] * (len(operands) - 1),
        out_specs=(whole,) * len(outputs),
        scratch_shapes=[pltpu.VMEM(x.shape, x.dtype) for x in scratch],
        compiler_params=pltpu.CompilerParams(vmem_limit_bytes=needed + spare * 1024 * 1024),
        cost_estimate=pl.CostEstimate(flops=1, bytes_accessed=1, transcendentals=0),
    )(*operands)


def shape(like, *dims):
    return jax.ShapeDtypeStruct(dims, like.dtype)


def span(index, size):
    return pl.ds(pl.multiple_of(index * size, size), size)


def squares_kernel(marks, hidden_ref, out_ref):
    values = hidden_ref[...].astype(jnp.float32)
    total = jnp.sum(values * values, axis=1, keepdims=True)
    out_ref[...] = jnp.broadcast_to(total, out_ref.shape)


def corners_kernel(features, marks, hidden_ref, gain_ref, sum_0, sum_1, along_xy, along_x, along_y, own):
    x, y = marks[X], marks[Y]
    rows, width = own.shape
    places = ((1 - x, 1 - y), (1 - x, y), (x, 1 - y), (x, y))
    for out, (h, side) in zip((along_xy, along_x, along_y, own), places):
        block = hidden_ref[span(h, rows), span(side, width)].astype(jnp.float32)
        gain = gain_ref[:, span(side, width)].astype(jnp.float32)
        mean = (sum_0[span(h, rows), 0:1] + sum_1[span(h, rows), 0:1]) / features
        out[...] = (block * lax.rsqrt(mean + norm_epsilon) * gain).astype(out.dtype)


def arrange_kernel(marks, w_ref, keep, send):
    zh, zl, y = marks[ZH], marks[ZL], marks[Y]
    for middle, out in ((1 - zl, send), (zl, keep)):
        for i, high in enumerate((1 - y, y)):
            for j, low in enumerate((1 - zh, zh)):
                at = (i * 2 + j) * HD
                out[:, at : at + HD] = w_ref[:, span(high * 4 + middle * 2 + low, HD)]


def arrange_out_kernel(marks, w_ref, keep, send):
    zh, zl = marks[ZH], marks[ZL]
    width = keep.shape[1]
    for out, mine in ((send, 1 - zl), (keep, zl)):
        for i in range(2):
            for j in range(2):
                at = i * 2 + j
                out[at * HD : (at + 1) * HD, :] = w_ref[
                    span(2 * (i ^ mine) + (j ^ zh), HD), span(mine, width)
                ]


def project_kernel(marks, *refs):
    first, second, send_out, keep_out = refs[-4:]
    inputs = refs[:-4]
    middle = first.shape[1] // 2
    for i in range(0, len(inputs), 2):
        rows = inputs[i].shape[0]
        into = pl.ds(i // 2 * rows, rows)
        for out, columns in ((send_out, pl.ds(0, middle)), (keep_out, pl.ds(middle, middle))):
            out[into, :] = (
                jnp.dot(inputs[i][...], first[:, columns], preferred_element_type=jnp.float32)
                + jnp.dot(
                    inputs[i + 1][...], second[:, columns], preferred_element_type=jnp.float32
                )
            ).astype(out.dtype)


def project(marks, pairs, first, second):
    inputs = [block for pair in pairs for block in pair]
    rows = sum(pair[0].shape[0] for pair in pairs)
    columns = first.shape[1]
    outputs = (
        jax.ShapeDtypeStruct((rows, columns // 2), jnp.bfloat16),
        jax.ShapeDtypeStruct((rows, columns // 2), jnp.float32),
    )
    return local_call(project_kernel, outputs, (marks, *inputs, first, second))


def out_kernel(
    marks, own_0, own_1, other_0, other_1, keep_ref, got_ref, send_0, send_1, keep_0, keep_1, joined
):
    part = own_0.shape[-2]
    depth = keep_ref.shape[0]
    aside = marks[ZL] ^ marks[CORE]
    for first in range(8):
        order = ((first & 3) << 1) | (first >> 2)
        row = (order ^ 7) ^ (marks[ZH] * 4 + marks[ZL] * 2 + marks[Y])
        for h, (own, other) in enumerate(((own_0, other_0), (own_1, other_1))):
            at = pl.ds((first * 2 + h) * part, part)
            for ref, place in ((own, aside), (other, 1 - aside)):
                for block in range(4):
                    joined[at, span(place * 4 + block, HD)] = ref[block >> 1, block & 1, row]
    rows, columns = send_0.shape
    for at, outs in ((0, (send_0, send_1)), (rows, (keep_0, keep_1))):
        for side, out in enumerate(outs):
            across = pl.ds(side * columns, columns)
            out[...] = (
                jnp.dot(
                    joined[at : at + rows, :depth],
                    keep_ref[:, across],
                    preferred_element_type=jnp.float32,
                )
                + jnp.dot(
                    joined[at : at + rows, depth:],
                    got_ref[:, across],
                    preferred_element_type=jnp.float32,
                )
            ).astype(out.dtype)


def home_kernel(marks, keep_ref, got_ref, out_ref):
    pieces, small = keep_ref.shape[2:4]
    for aside, ref in enumerate((keep_ref, got_ref)):
        for block in range(4):
            zl, zh = block >> 1, block & 1
            head = (marks[Y] ^ aside) * 4 + (marks[ZL] ^ zl) * 2 + (marks[ZH] ^ zh)
            for piece in range(pieces):
                out_ref[piece * small : (piece + 1) * small, span(head, HD)] = ref[zl, zh, piece]


def finish_kernel(marks, hidden_ref, *refs):
    out_ref = refs[-1]
    rows, width = refs[0].shape
    part = rows // 2
    for j in range(2):
        for place, ref in ((marks[ZL], refs[2 * j]), (1 - marks[ZL], refs[2 * j + 1])):
            for h in range(2):
                at = span((h ^ marks[X]) * 2 + j, part)
                block = hidden_ref[at, span(place, width)].astype(jnp.float32)
                added = ref[h * part : (h + 1) * part, :].astype(jnp.float32)
                out_ref[at, span(place, width)] = (block + added).astype(out_ref.dtype)


def after(values, *earlier):
    return lax.optimization_barrier((values, *earlier))[0]


def on_device_paired(hidden, norm_gain, w_query, w_key, w_value, w_out):
    rows, cols = lax.axis_size("row"), lax.axis_size("col")
    tokens, width = hidden.shape[0], hidden.shape[1] // 2
    length = tokens * rows
    row, col = lax.axis_index("row"), lax.axis_index("col")
    y, zl, zh = row & 1, (row >> 1) & 1, row >> 2
    core, x = col & 1, col >> 1
    marks = jnp.stack((x, core, zh, zl, y)).astype(jnp.int32)
    steps = {"y": (1, 0), "zl": (2, 0), "zh": (4, 0), "core": (0, 1), "x": (0, 2), "xy": (1, 2)}

    def swap(values, name):
        by_row, by_col = steps[name]
        pairs = [
            (r * cols + c, (r ^ by_row) * cols + (c ^ by_col))
            for r in range(rows)
            for c in range(cols)
        ]
        return lax.ppermute(values, ("row", "col"), pairs)

    def spread(block, along, *earlier):
        held = jnp.concatenate((block, along))
        beside = swap(after(held, *earlier), "x")
        return held, swap(held, "core"), beside

    def ordered(mine, other, bit):
        return jnp.where(bit == 0, mine, other), jnp.where(bit == 0, other, mine)

    def index(values, at, axis=0):
        return lax.dynamic_index_in_dim(values, at, axis, keepdims=False)

    def halves(values):
        middle = values.shape[0] // 2
        return values[:middle], values[middle:]

    sums_shape = jax.ShapeDtypeStruct((tokens, HD), jnp.float32)
    (squares,) = local_call(squares_kernel, (sums_shape,), (marks, hidden))
    depth = w_value.shape[0]

    def arranged(weight, *earlier):
        half = shape(weight, depth, 4 * HD)
        return local_call(arrange_kernel, (half, half), (after(marks, *earlier), weight))

    v_keep, v_send = arranged(w_value)
    v_got = swap(v_send, "zl")
    squares = squares + swap(squares, "core")
    squares = after(squares, v_send)
    squares_x = swap(squares, "x")

    quarter = shape(hidden, tokens // 2, width)
    to_xy, to_x, to_y, own = local_call(
        functools.partial(corners_kernel, hidden.shape[1] * cols),
        (quarter,) * 4,
        (marks, hidden, norm_gain.reshape(1, -1), squares, squares_x),
    )
    from_xy, from_x, from_y = swap(to_xy, "xy"), swap(to_x, "x"), swap(to_y, "y")

    mine = jnp.concatenate(ordered(own, from_y, y))
    theirs = jnp.concatenate(ordered(from_x, from_xy, y))
    block_a, send = ordered(mine, theirs, x ^ zh)
    along_a = swap(after(block_a, v_got), "zl")
    block_b = swap(after(send, along_a), "zh")

    k_keep, k_send = arranged(w_key, to_y)
    q_keep, q_send = arranged(w_query, to_y)
    positions = jnp.arange(length, dtype=jnp.int32)
    cosine, sine = turning(after(positions, to_y))
    out_depth, out_width = w_out.shape
    half = shape(w_out, out_depth, out_width // 2)
    out_keep, out_send = local_call(arrange_out_kernel, (half, half), (after(marks, to_y), w_out))

    along_a = after(along_a, k_send, q_send, cosine, sine, out_send)
    k_got = swap(after(k_send, along_a), "zl")
    held_a, core_a, beside_a = spread(block_a, along_a)
    pairs_a = ((held_a, core_a), (beside_a, swap(beside_a, "core")))
    along_b = swap(block_b, "zl")
    held_b, core_b, beside_b = spread(block_b, along_b, beside_a)
    q_got = swap(after(q_send, k_got), "zl")

    def multiply(pairs, keep, got, *earlier):
        return project(after(marks, *earlier), pairs, *ordered(keep, got, zl ^ core))

    weights = ((v_keep, v_got), (k_keep, k_got), (q_keep, q_got))
    products = [multiply(pairs_a, *weights[0])]
    products.append(multiply(pairs_a, *weights[1], products[0][0]))
    sums, kept, got = [], [], []
    for i in range(6):
        if i == 1:
            products.append(multiply(pairs_a, *weights[2], sums[0]))
            beside_b = after(beside_b, products[1][0])
            pairs_b = ((held_b, core_b), (beside_b, swap(beside_b, "core")))
        if 2 <= i < 5:
            products.append(multiply(pairs_b, *weights[i - 2], sums[i - 1]))
        send, keep = products[i]
        if i >= 2:
            send = after(send, sums[i - 2])
            keep = after(keep, *(got[i - 2 : i - 1] if i >= 3 else ()))
        if i < 5:
            keep = after(keep, products[i + 1][0])
        total = keep + swap(send, "y").astype(jnp.float32)
        sums.append(total[:, :HD].astype(jnp.bfloat16))
        kept.append(total[:, HD:])
        got.append(swap(sums[-1], "zh"))

    value, key, query = (
        jnp.concatenate((kept[a] + got[b].astype(jnp.float32), kept[b] + got[a].astype(jnp.float32)))
        .reshape(-1, tokens // 2, HD)
        for a, b in ((0, 3), (1, 4), (2, 5))
    )
    context = attention(marks, query, key, value, cosine, sine)
    pieces, _, small, _ = context.shape

    out_got = swap(after(out_send, q_got), "zl")
    context = after(context, out_got)

    sides = context.reshape(2, pieces // 2, rows, small, HD)
    outward = index(sides, 1 - x)
    held, crossed = [], []
    for j in range(pieces // 2):
        near, send = ordered(index(sides, x)[j], swap(outward[j], "x"), x ^ zh)
        held.append(near)
        crossed.append(swap(send, "zh"))
    blocks = [jnp.stack((held[j], crossed[j])) for j in range(pieces // 2)]
    alongs = [swap(block, "zl") for block in blocks]
    sums, got, mine, theirs, finals = [], [], [], [], []
    count = rows * small
    outputs = (jax.ShapeDtypeStruct((count, out_width // 4), jnp.bfloat16),) * 2
    outputs += (jax.ShapeDtypeStruct((count, out_width // 4), jnp.float32),) * 2
    products = []
    for block, along in zip(blocks, alongs):
        block = jnp.stack((block, along))
        beside = swap(block, "x")
        further = swap(after(beside, alongs[-1], *(sent[0] for sent in products)), "core")
        products.append(
            local_call(
                out_kernel,
                outputs,
                (marks, block, beside, swap(block, "core"), further, out_keep, out_got),
                scratch=[jax.ShapeDtypeStruct((2 * count, 2 * out_depth), jnp.bfloat16)],
            )
        )
    first, second = products
    block = after(context, first[0]).reshape(pieces, 2, 2, 2, small, HD)
    home = jnp.stack((index(block, zh, 1), swap(index(block, 1 - zh, 1), "zh")))
    for i, (send, keep) in enumerate(
        ((first[0], first[2]), (first[1], first[3]), (second[0], second[2]), (second[1], second[3]))
    ):
        if i == 1:
            keep = after(keep, home)
        if i == 3:
            home = jnp.stack((index(home, zl, 2), swap(index(home, 1 - zl, 2), "zl")))
            keep = after(keep, home)
        if i >= 2:
            send = after(send, sums[i - 2])
        if i >= 3:
            send = after(send, got[i - 3])
        total = keep + swap(send, "y").astype(jnp.float32)
        send, keep = halves(total)
        sums.append(send.astype(jnp.bfloat16))
        got.append(swap(sums[-1], "zh"))
        send, keep = halves((keep + got[-1].astype(jnp.float32)).astype(jnp.bfloat16))
        theirs.append(send)
        mine.append(keep)
        if i & 1:
            finals.append(jnp.concatenate(mine[-2:], axis=1))
            finals.append(swap(jnp.concatenate(theirs[-2:], axis=1), "zl"))

    home = after(home, sums[3])
    (context_out,) = local_call(
        home_kernel,
        (shape(hidden, tokens, rows * HD),),
        (marks, index(home, y, 3), swap(index(home, 1 - y, 3), "y")),
    )
    (layer_out,) = local_call(
        finish_kernel, (shape(hidden, *hidden.shape),), (marks, hidden, *finals)
    )
    return (context_out, layer_out)


def on_device(hidden, norm_gain, w_query, w_key, w_value, w_out):
    rows, cols = lax.axis_size("row"), lax.axis_size("col")
    heads_here = w_query.shape[1] // HD
    paired = rows == 2**3 and cols == 2**2 and heads_here == rows and hidden.shape[0] % 64 == 0
    plan = on_device_paired if paired else on_device_any
    return plan(hidden, norm_gain, w_query, w_key, w_value, w_out)


def solution(mesh):
    placed = (
        P("row", "col"),
        P("col"),
        P("row", "col"),
        P("row", "col"),
        P("row", "col"),
        P("row", "col"),
    )
    return jax.shard_map(
        on_device,
        mesh=mesh,
        in_specs=placed,
        out_specs=(P("row", "col"), P("row", "col")),
        check_vma=False,
    )
```
